32 devices in a mesh: groups: 2 (over x), tensor: 8 (over z, y), section: 2 (over core).
Axes of the slice: x: 2, y: 2, z: 4, core: 2. Of those that a mesh axis runs over, the one named last changes fastest.
Arguments:
- prefill_queries: bfloat16 [2, 4096, 8192], P('section', ('groups', 'tensor')), parts along dimension 1, may hold values from -26 to 26
- prefill_key_values: bfloat16 [2, 4096, 2048], P('section', ('groups', 'tensor')), parts along dimension 1, may hold values from -6 to 6
- decode_step_queries: bfloat16 [256, 8192], P(('groups', 'tensor', 'section')), parts along dimension 0, may hold values from -26 to 26
- cached_page_pool: bfloat16 [2048, 4, 2048], P(('groups', 'tensor', 'section')), parts along dimension 0, may hold values from -6 to 6
- trajectory_page_table: int32 [256, 8], P(('groups', 'tensor', 'section')), parts along dimension 0, may hold values from 0 to 63, as said below
- lengths: int32 [256], P(('groups', 'tensor', 'section')), parts along dimension 0, may hold values from 2 to 32, as said below
- page_owner: int32 [2, 1024], P(None, 'groups'), parts along dimension 1, may hold values from 0 to 15, as said below
- page_slot: int32 [2, 1024], P(None, 'groups'), parts along dimension 1, may hold values from 0 to 7
Outputs:
- stretch_context: bfloat16 [2, 4096, 8192], P('section', ('groups', 'tensor')), parts along dimension 1
- step_context: bfloat16 [256, 8192], P(('groups', 'tensor', 'section')), parts along dimension 0
The draws below stay inside these ranges and needn't reach their ends.
There are 2 independent parts, one for each index of `groups`. The reference program is written for one: setup_inputs(seed, part) draws one part's arguments, and reference() takes and returns one part's arrays. A program takes and returns all parts, laid end to end along the dimension named above; each array names one. Nothing has to cross between parts.
Inputs may be any that keep to these rules, and one draw needn't show every extreme that they name: `page_owner`: cut each stretch's 512 pages into blocks of 512 consecutive pages: no owner is named by more than 64 pages of one block, and one owner is named by exactly 64 pages of every block. `trajectory_page_table`: the rows of the 8 trajectories of one owner together name each of its 64 slots exactly once. `lengths`: every owner has a trajectory of length 32.
All inputs are finite; a program needn't handle non-finite values.
Results may differ from the reference program's by a relative error of at most 0.004.
Values may be sent and summed in bfloat16 or wider, within the bound.
A program may use at most 320 MiB of HBM per device.

```python
import math
import jax
import jax.numpy as jnp
from jax import lax

QUERY_HEADS = 64
KEY_VALUE_HEADS = 8
HEAD_SIZE = 128
STRETCH_TOKENS = 2048
PAGE_TOKENS = 4
OWNER_TRAJS = 8
MAX_TRAJ_PAGES = 8
STRETCH_COUNT = 2
QUERY_PER_KEY = 8
QUARTERS = 1
NPAGES = 512
PAGES_BLOCK = 512
OWNERS = 16
CAP = 64
TRAJECTORY_COUNT = 128
OLD_SLOTS = 64
POOL_SLOTS = 1024


def blended_normal(key, shape):
    first_key = jax.random.fold_in(key, 0)
    normal = jnp.clip(jax.random.normal(first_key, shape, jnp.float32), -6.0, 6.0)
    return normal


def table_of(key):
    key = jax.random.fold_in(key, 71)
    scores = jax.random.randint(key, (OWNERS, OLD_SLOTS), 0, 65536) * OLD_SLOTS + jnp.arange(OLD_SLOTS, dtype=jnp.int32)[None, :]
    slot_order = jnp.argsort(scores, axis=1).astype(jnp.int32)
    return slot_order.reshape(TRAJECTORY_COUNT, MAX_TRAJ_PAGES)


def cache_of(key, blend_weight):
    page_table_rows = table_of(key)
    key = jax.random.fold_in(key, 29)
    root_random_key = jax.random.fold_in(key, 0)
    pool_entries = blended_normal(root_random_key, (POOL_SLOTS, PAGE_TOKENS, KEY_VALUE_HEADS, 2, HEAD_SIZE))
    first_page = jnp.arange(TRAJECTORY_COUNT, dtype=jnp.int32) // OWNER_TRAJS * OLD_SLOTS + page_table_rows[:, 0]
    first_mark = jnp.zeros((POOL_SLOTS,), jnp.float32).at[first_page].set(1.0)
    weight_map = blend_weight * first_mark[:, None, None]
    first_row = (1.0 - weight_map) * pool_entries[:, 0, :, 0]
    second_row = (1.0 - weight_map) * pool_entries[:, 1, :, 0]
    pool_entries = pool_entries.at[:, 0, :, 0].set(first_row).at[:, 1, :, 0].set(second_row)
    return pool_entries


def stretch_of(key):
    key = jax.random.fold_in(key, 41)
    root_random_key = jax.random.fold_in(key, 0)
    key_value_entries = blended_normal(root_random_key, (STRETCH_COUNT, STRETCH_TOKENS, KEY_VALUE_HEADS, 2, HEAD_SIZE))
    first_row = key_value_entries[:, 0, :, 0]
    second_row = key_value_entries[:, 1, :, 0]
    key_value_entries = key_value_entries.at[:, 0, :, 0].set(first_row).at[:, 1, :, 0].set(second_row)
    return key_value_entries


def draw_prefill_key_values(key, part):
    key_value_entries = stretch_of(key)
    return key_value_entries.reshape(STRETCH_COUNT, STRETCH_TOKENS, 2 * KEY_VALUE_HEADS * HEAD_SIZE).astype(jnp.bfloat16)


def draw_prefill_queries(key, part):
    blend_weight = 0.0
    key = jax.random.fold_in(key, 13)
    base_offset = blended_normal(key, (STRETCH_COUNT, STRETCH_TOKENS, KEY_VALUE_HEADS, QUERY_PER_KEY, HEAD_SIZE))
    row_ids = jnp.arange(STRETCH_TOKENS, dtype=jnp.int32)
    weight_map = blend_weight * (row_ids % 61 == 7).astype(jnp.float32)[None, :, None, None, None]
    query_vectors = (1.0 - weight_map) * base_offset
    return query_vectors.reshape(STRETCH_COUNT, STRETCH_TOKENS, QUERY_HEADS * HEAD_SIZE).astype(jnp.bfloat16)


def draw_cached_page_pool(key, part):
    blend_weight = 0.0
    pool_entries = cache_of(key, blend_weight)
    return pool_entries.reshape(POOL_SLOTS, PAGE_TOKENS, 2 * KEY_VALUE_HEADS * HEAD_SIZE).astype(jnp.bfloat16)


def draw_decode_step_queries(key, part):
    blend_weight = 0.0
    key = jax.random.fold_in(key, 17)
    base_offset = blended_normal(key, (TRAJECTORY_COUNT, KEY_VALUE_HEADS, QUERY_PER_KEY, HEAD_SIZE))
    row_ids = jnp.arange(TRAJECTORY_COUNT, dtype=jnp.int32)
    weight_map = blend_weight * (row_ids % 3 == 0).astype(jnp.float32)[:, None, None, None]
    query_vectors = (1.0 - weight_map) * base_offset
    return query_vectors.reshape(TRAJECTORY_COUNT, QUERY_HEADS * HEAD_SIZE).astype(jnp.bfloat16)


def draw_trajectory_page_table(key, part):
    page_table_rows = table_of(key)
    return page_table_rows


def draw_lengths(key, part):
    key = jax.random.fold_in(key, 7)
    first_key, second_key = jax.random.split(key)
    base_offset = jax.random.randint(first_key, (OWNERS, OWNER_TRAJS), 2, MAX_TRAJ_PAGES * PAGE_TOKENS + 1)
    longest = jax.random.randint(second_key, (OWNERS, 1), 0, OWNER_TRAJS)
    filled = jnp.where(jnp.arange(OWNER_TRAJS, dtype=jnp.int32)[None, :] == longest, MAX_TRAJ_PAGES * PAGE_TOKENS, base_offset)
    return filled.reshape(TRAJECTORY_COUNT).astype(jnp.int32)


def draw_page_owner(key, part):
    key = jax.random.fold_in(key, 3)
    full_key, block_key = jax.random.split(key)
    full_owner = jax.random.randint(full_key, (), 0, OWNERS)
    token_count = OWNERS * CAP
    owner_tokens = jnp.arange(token_count, dtype=jnp.int32) // CAP

    def one_block(sub_key):
        rank_key, shuffle_key = jax.random.split(sub_key)
        scores = jax.random.randint(rank_key, (token_count,), 0, 1 << 20) * token_count + jnp.arange(token_count, dtype=jnp.int32)
        scores = jnp.where(owner_tokens == full_owner, -1, scores)
        chosen = owner_tokens[jnp.argsort(scores)[:PAGES_BLOCK]]
        return chosen[jax.random.permutation(shuffle_key, PAGES_BLOCK)]
    block_keys = jax.random.split(block_key, STRETCH_COUNT * QUARTERS)
    return jax.vmap(one_block)(block_keys).reshape(STRETCH_COUNT, NPAGES).astype(jnp.int32)


def place_ends(result, stream_key, low, high):
    spot = [jax.random.randint(jax.random.fold_in(stream_key, axis), (), 0, length) for axis, length in enumerate(result.shape)]
    widest = result.shape.index(max(result.shape))
    neighbour = spot[:widest] + [(spot[widest] + 1) % result.shape[widest]] + spot[widest + 1:]
    return result.at[tuple(spot)].set(low).at[tuple(neighbour)].set(high)


def setup_inputs(seed: int = 0, part: int = 0) -> dict:
    key_list = jax.random.split(jax.random.key(seed), 9)
    part_splits = jax.random.split(jax.random.fold_in(key_list[8], part), 9)
    prefill_queries = draw_prefill_queries(jax.random.fold_in(jax.random.fold_in(key_list[8], part), 71), part)
    prefill_key_values = draw_prefill_key_values(jax.random.fold_in(jax.random.fold_in(key_list[8], part), 71), part)
    decode_step_queries = draw_decode_step_queries(jax.random.fold_in(jax.random.fold_in(key_list[8], part), 71), part)
    cached_page_pool = draw_cached_page_pool(jax.random.fold_in(jax.random.fold_in(key_list[8], part), 71), part)
    trajectory_page_table = draw_trajectory_page_table(jax.random.fold_in(jax.random.fold_in(key_list[8], part), 71), part)
    lengths = draw_lengths(jax.random.fold_in(jax.random.fold_in(key_list[8], part), 71), part)
    page_owner = draw_page_owner(jax.random.fold_in(jax.random.fold_in(key_list[8], part), 71), part)
    page_slot = place_ends(jax.random.randint(part_splits[7], (STRETCH_COUNT, NPAGES), 0, OWNER_TRAJS), jax.random.fold_in(part_splits[7], 1), 0, OWNER_TRAJS - 1).astype(jnp.int32)
    return dict(prefill_queries=prefill_queries, prefill_key_values=prefill_key_values, decode_step_queries=decode_step_queries, cached_page_pool=cached_page_pool, trajectory_page_table=trajectory_page_table, lengths=lengths, page_owner=page_owner, page_slot=page_slot)


def stretch_attention(query_vectors, key_value_rows):
    query_head_count = query_vectors.reshape(STRETCH_TOKENS, KEY_VALUE_HEADS, QUERY_PER_KEY, HEAD_SIZE)
    key_value_pairs = key_value_rows.reshape(STRETCH_TOKENS, KEY_VALUE_HEADS, 2, HEAD_SIZE)
    causal = jnp.arange(STRETCH_TOKENS)[:, None] >= jnp.arange(STRETCH_TOKENS)[None, :]
    scaling = 1.0 / math.sqrt(HEAD_SIZE)

    def single_head(kv_index):
        head_queries = lax.dynamic_index_in_dim(query_head_count, kv_index, 1, keepdims=False).astype(jnp.float32)
        head_pairs = lax.dynamic_index_in_dim(key_value_pairs, kv_index, 1, keepdims=False)
        key_part = head_pairs[:, 0].astype(jnp.float32)
        value_part = head_pairs[:, 1].astype(jnp.float32)
        scores = jnp.einsum('igd,jd->gij', head_queries, key_part) * scaling
        scores = jnp.where(causal[None], scores, -jnp.inf)
        row_top = lax.optimization_barrier(jnp.max(scores, axis=-1, keepdims=True))
        exp_terms = jnp.exp(scores - row_top)
        totals = lax.optimization_barrier(jnp.sum(exp_terms, axis=-1))
        rounded = lax.optimization_barrier(exp_terms.astype(jnp.bfloat16)).astype(jnp.float32)
        mixture = jnp.einsum('gij,jd->igd', rounded, value_part)
        return mixture / jnp.transpose(totals)[:, :, None]
    each_head_rows = lax.map(single_head, jnp.arange(KEY_VALUE_HEADS, dtype=jnp.int32))
    return jnp.transpose(each_head_rows, (1, 0, 2, 3)).reshape(STRETCH_TOKENS, QUERY_HEADS * HEAD_SIZE).astype(jnp.bfloat16)

def reference(prefill_queries, prefill_key_values, decode_step_queries, cached_page_pool, trajectory_page_table, lengths, page_owner, page_slot):
    stretch_context = jnp.stack([stretch_attention(prefill_queries[index], prefill_key_values[index]) for index in range(STRETCH_COUNT)])
    fresh_key_value_pairs = prefill_key_values.reshape(STRETCH_COUNT * STRETCH_TOKENS, KEY_VALUE_HEADS, 2, HEAD_SIZE)
    new_keys = fresh_key_value_pairs[:, :, 0].astype(jnp.float32)
    new_values = fresh_key_value_pairs[:, :, 1].astype(jnp.float32)
    target = (page_owner * OWNER_TRAJS + page_slot).reshape(STRETCH_COUNT * NPAGES)
    target_rows = jnp.repeat(target, PAGE_TOKENS)
    scaling = 1.0 / math.sqrt(HEAD_SIZE)

    def one_owner(owner_id):
        first_position = owner_id * OWNER_TRAJS
        query_vectors = lax.dynamic_slice_in_dim(decode_step_queries, first_position, OWNER_TRAJS, 0).reshape(OWNER_TRAJS, KEY_VALUE_HEADS, QUERY_PER_KEY, HEAD_SIZE).astype(jnp.float32)
        page_table_rows = lax.dynamic_slice_in_dim(trajectory_page_table, first_position, OWNER_TRAJS, 0)
        length_rows = lax.dynamic_slice_in_dim(lengths, first_position, OWNER_TRAJS, 0)
        pool_page_array = lax.dynamic_slice_in_dim(cached_page_pool, owner_id * OLD_SLOTS, OLD_SLOTS, 0)
        previous_pages = pool_page_array[page_table_rows].reshape(OWNER_TRAJS, MAX_TRAJ_PAGES * PAGE_TOKENS, KEY_VALUE_HEADS, 2, HEAD_SIZE)
        old_mask = jnp.arange(MAX_TRAJ_PAGES * PAGE_TOKENS, dtype=jnp.int32)[None, :] < length_rows[:, None]
        new_mask = target_rows[None, :] == (first_position + jnp.arange(OWNER_TRAJS, dtype=jnp.int32))[:, None]
        old_scores = jnp.einsum('tkgd,tnkd->tkgn', query_vectors, previous_pages[:, :, :, 0].astype(jnp.float32)) * scaling
        new_scores = jnp.einsum('tkgd,nkd->tkgn', query_vectors, new_keys) * scaling
        old_scores = jnp.where(old_mask[:, None, None, :], old_scores, -jnp.inf)
        new_scores = jnp.where(new_mask[:, None, None, :], new_scores, -jnp.inf)
        row_top = jnp.maximum(lax.optimization_barrier(jnp.max(old_scores, axis=-1)), lax.optimization_barrier(jnp.max(new_scores, axis=-1)))[..., None]
        old_terms = jnp.exp(old_scores - row_top)
        new_terms = jnp.exp(new_scores - row_top)
        totals = lax.optimization_barrier(jnp.sum(old_terms, axis=-1)) + lax.optimization_barrier(jnp.sum(new_terms, axis=-1))
        old_round = lax.optimization_barrier(old_terms.astype(jnp.bfloat16)).astype(jnp.float32)
        new_round = lax.optimization_barrier(new_terms.astype(jnp.bfloat16)).astype(jnp.float32)
        mixture = jnp.einsum('tkgn,tnkd->tkgd', old_round, previous_pages[:, :, :, 1].astype(jnp.float32))
        mixture = mixture + jnp.einsum('tkgn,nkd->tkgd', new_round, new_values)
        mixture = mixture / totals[..., None]
        return mixture.reshape(OWNER_TRAJS, QUERY_HEADS * HEAD_SIZE).astype(jnp.bfloat16)
    step_context = lax.map(one_owner, jnp.arange(OWNERS, dtype=jnp.int32)).reshape(TRAJECTORY_COUNT, QUERY_HEADS * HEAD_SIZE)
    return (stretch_context, step_context)
```

```python
import functools
import math

import jax
import jax.numpy as jnp
from jax import lax
from jax.experimental import pallas as pl
from jax.experimental.pallas import tpu as pltpu
from jax.sharding import PartitionSpec as P

QUERY_HEADS = 64
KEY_VALUE_HEADS = 8
HEAD_SIZE = 128
PAGE_TOKENS = 4
GROUP = QUERY_HEADS // KEY_VALUE_HEADS
NEG = -1e30
EXP2_SCALE = math.log2(math.e) / math.sqrt(HEAD_SIZE)
MESH = pl.DeviceIdType.MESH
CHUNK_HEADS = 2
CHUNKS = KEY_VALUE_HEADS // CHUNK_HEADS
HALF = CHUNKS // 2
CHUNK_COLS = CHUNK_HEADS * 2 * HEAD_SIZE


def ring_place(index, n):
    if n != 8:
        return index
    odd = index % 2
    return (index // 2) * (1 - odd) + (n - 1 - index // 2) * odd


def ring_device(place, n):
    place = (place + 2 * n) % n
    if n != 8:
        return place
    far = place // (n // 2)
    return (2 * place) * (1 - far) + (2 * (n - 1 - place) + 1) * far


def scores_t(k, q):
    return lax.dot_general(k, q, (((1,), (1,)), ((), ())), preferred_element_type=jnp.float32)


def flash(s, vt, acc_ref, m_ref, l_ref, h, first):
    top = jnp.max(s, axis=0, keepdims=True)
    if not first:
        old = m_ref[h, 0:1]
        top = jnp.maximum(top, old)
    p = jnp.exp2((s - top) * EXP2_SCALE)
    total = jnp.sum(p, axis=0, keepdims=True)
    mix = jnp.dot(vt, p.astype(jnp.bfloat16), preferred_element_type=jnp.float32)
    if not first:
        alpha = jnp.exp2((old - top) * EXP2_SCALE)
        total = total + l_ref[h, 0:1] * alpha
        mix = mix + acc_ref[h] * alpha
    m_ref[h, 0:1] = top
    l_ref[h, 0:1] = total
    acc_ref[h] = mix


def kernel(
    n,
    q_ref,
    kv_ref,
    pool_ref,
    dq_ref,
    bias_ref,
    old_bias_ref,
    out_ref,
    dec_ref,
    kvs,
    acc,
    m_sc,
    l_sc,
    dacc,
    dm,
    dl,
    dsib,
    dqs,
    xsend,
    xrecv,
    send_sem,
    recv_sem,
    pair_send,
    pair_recv,
):
    rows = q_ref.shape[0]
    steps = dq_ref.shape[1]
    me = lax.axis_index("tensor")
    place = ring_place(me, n)
    right = ring_device(place + 1, n)
    left = ring_device(place - 1, n)
    sibling = 1 - lax.axis_index("section")

    barrier = pltpu.get_barrier_semaphore()
    for target in ({"tensor": right}, {"tensor": left}, {"section": sibling}):
        pl.semaphore_signal(barrier, inc=1, device_id=target, device_id_type=MESH)
    pl.semaphore_wait(barrier, 3)

    def ring_copy(src, slot, chunk, step, target):
        return pltpu.make_async_remote_copy(
            src_ref=src,
            dst_ref=kvs.at[slot, chunk],
            send_sem=send_sem.at[step * CHUNKS + chunk],
            recv_sem=recv_sem.at[step * CHUNKS + chunk],
            device_id={"tensor": target},
            device_id_type=MESH,
        )

    def pair_copy(src, dst, which):
        return pltpu.make_async_remote_copy(
            src_ref=src,
            dst_ref=dst,
            send_sem=pair_send.at[which],
            recv_sem=pair_recv.at[which],
            device_id={"section": sibling},
            device_id_type=MESH,
        )

    for c in range(HALF):
        for chunk, target in ((c, right), (HALF + c, left)):
            kvs[me, chunk] = kv_ref[:, chunk * CHUNK_COLS : (chunk + 1) * CHUNK_COLS]
            ring_copy(kvs.at[me, chunk], me, chunk, 0, target).start()
    swap_queries = pair_copy(dq_ref, dsib, 0)
    swap_queries.start()

    causal = lax.broadcasted_iota(jnp.int32, (rows, rows), 1) >= lax.broadcasted_iota(
        jnp.int32, (rows, rows), 0
    )

    def query_head(h):
        return q_ref[:, pl.ds(pl.multiple_of(h * HEAD_SIZE, HEAD_SIZE), HEAD_SIZE)]

    def attend(k, vt, g, first):
        s = scores_t(k, query_head(g * GROUP))
        for j in range(GROUP):
            following = scores_t(k, query_head(g * GROUP + j + 1)) if j + 1 < GROUP else None
            if first:
                s = jnp.where(causal, s, NEG)
            flash(s, vt, acc, m_sc, l_sc, g * GROUP + j, first)
            s = following

    def kv_cols(ref, g):
        start = pl.multiple_of(g * 2 * HEAD_SIZE, 2 * HEAD_SIZE)
        return (
            ref[:, pl.ds(start, HEAD_SIZE)],
            ref[:, pl.ds(pl.multiple_of(start + HEAD_SIZE, HEAD_SIZE), HEAD_SIZE)],
        )

    swap_queries.wait()
    for g in range(KEY_VALUE_HEADS):
        dqs[g, 0:steps] = dq_ref[g]
        dqs[g, steps : 2 * steps] = dsib[g]
        start = g * 2 * HEAD_SIZE
        k = pool_ref[:, start : start + HEAD_SIZE]
        v = pool_ref[:, start + HEAD_SIZE : start + 2 * HEAD_SIZE]
        s = scores_t(k, dqs[g]) + old_bias_ref[...]
        flash(s, jnp.transpose(v), dacc, dm, dl, g, True)

    def own_head(g, carry):
        k, v = kv_cols(kv_ref, g)
        vt = jnp.transpose(v)
        s = scores_t(k, dqs[g]) + bias_ref[me]
        flash(s, vt, dacc, dm, dl, g, False)
        attend(k, vt, g, True)
        return carry

    lax.fori_loop(0, KEY_VALUE_HEADS, own_head, 0)

    def ring_step(step, carry):
        src_right = ring_device(place - step, n)
        src_left = ring_device(place + step, n)

        def part(c, carry):
            for chunk, slot, target in ((c, src_right, right), (HALF + c, src_left, left)):
                block = kvs.at[slot, chunk]
                ring_copy(block, slot, chunk, step - 1, target).wait_recv()

                @pl.when(step < n - 1)
                def _():
                    ring_copy(block, slot, chunk, step, target).start()

            def unit(u, carry):
                way = u // CHUNK_HEADS
                inner = u % CHUNK_HEADS
                chunk = way * HALF + c
                slot = src_right * (1 - way) + src_left * way
                g = chunk * CHUNK_HEADS + inner
                start = pl.multiple_of(inner * 2 * HEAD_SIZE, 2 * HEAD_SIZE)
                k = kvs[slot, chunk, :, pl.ds(start, HEAD_SIZE)]
                v = kvs[
                    slot, chunk, :, pl.ds(pl.multiple_of(start + HEAD_SIZE, HEAD_SIZE), HEAD_SIZE)
                ]
                vt = jnp.transpose(v)
                s = scores_t(k, dqs[g]) + bias_ref[slot]
                flash(s, vt, dacc, dm, dl, g, False)

                @pl.when(slot < me)
                def _():
                    attend(k, vt, g, False)

                return carry

            return lax.fori_loop(0, 2 * CHUNK_HEADS, unit, carry)

        return lax.fori_loop(0, HALF, part, carry)

    lax.fori_loop(1, n, ring_step, 0)

    def columns(row):
        return jnp.transpose(jnp.broadcast_to(row, (HEAD_SIZE, 2 * steps)))

    def stage(g, carry):
        xsend[g, 0] = jnp.transpose(dacc[g])[steps:]
        xsend[g, 1] = columns(dm[g, 0:1])[steps:]
        xsend[g, 2] = columns(dl[g, 0:1])[steps:]
        return carry

    lax.fori_loop(0, KEY_VALUE_HEADS, stage, 0)
    swap_parts = pair_copy(xsend, xrecv, 1)
    swap_parts.start()

    def finish(h, carry):
        mix = acc[h] / l_sc[h, 0:1]
        out_ref[:, pl.ds(pl.multiple_of(h * HEAD_SIZE, HEAD_SIZE), HEAD_SIZE)] = jnp.transpose(
            mix
        ).astype(jnp.bfloat16)
        return carry

    lax.fori_loop(0, QUERY_HEADS, finish, 0)
    swap_parts.wait()
    trajs = steps // GROUP
    for g in range(KEY_VALUE_HEADS):
        o_own = jnp.transpose(dacc[g])[:steps]
        m_own = columns(dm[g, 0:1])[:steps]
        l_own = columns(dl[g, 0:1])[:steps]
        top = jnp.maximum(m_own, xrecv[g, 1])
        w_own = jnp.exp2((m_own - top) * EXP2_SCALE)
        w_sib = jnp.exp2((xrecv[g, 1] - top) * EXP2_SCALE)
        mix = (o_own * w_own + xrecv[g, 0] * w_sib) / (l_own * w_own + xrecv[g, 2] * w_sib)
        for j in range(GROUP):
            col = (g * GROUP + j) * HEAD_SIZE
            dec_ref[:, col : col + HEAD_SIZE] = mix[j * trajs : (j + 1) * trajs].astype(
                jnp.bfloat16
            )

    def drain(step, carry):
        for c in range(HALF):
            for chunk, target in ((c, right), (HALF + c, left)):
                ring_copy(kvs.at[me, chunk], me, chunk, step, target).wait_send()
        return carry

    lax.fori_loop(0, n - 1, drain, 0)


def on_device(
    prefill_queries,
    prefill_key_values,
    decode_step_queries,
    cached_page_pool,
    trajectory_page_table,
    lengths,
    page_owner,
    page_slot,
):
    n = lax.axis_size("tensor")
    sections = lax.axis_size("section")
    me = lax.axis_index("tensor")
    section = lax.axis_index("section")
    rows = prefill_queries.shape[1]
    trajs = decode_step_queries.shape[0]
    steps = trajs * GROUP
    old_rows = cached_page_pool.shape[0] * PAGE_TOKENS
    q = prefill_queries[0]
    kv = prefill_key_values[0]
    pool = cached_page_pool.reshape(old_rows, cached_page_pool.shape[2])
    dq = (
        decode_step_queries.reshape(trajs, KEY_VALUE_HEADS, GROUP, HEAD_SIZE)
        .transpose(1, 2, 0, 3)
        .reshape(KEY_VALUE_HEADS, steps, HEAD_SIZE)
    )
    lanes = jnp.arange(2 * steps, dtype=jnp.int32)
    lane_traj = lanes % trajs
    lane_owner = me * sections + jnp.where(lanes < steps, section, 1 - section)
    target = lax.dynamic_index_in_dim(page_owner * trajs + page_slot, section, 0, keepdims=False)
    target = jnp.repeat(target, PAGE_TOKENS)
    bias = jnp.where(
        target[:, None] == (lane_owner * trajs + lane_traj)[None, :], 0.0, NEG
    ).astype(jnp.float32)
    bias = bias.reshape(n, rows, 2 * steps)
    slots = cached_page_pool.shape[0]
    pages = trajectory_page_table.shape[1]
    named = trajectory_page_table[None] == jnp.arange(slots, dtype=jnp.int32)[:, None, None]
    left_tokens = lengths[:, None] - jnp.arange(pages, dtype=jnp.int32)[None, :] * PAGE_TOKENS
    count = jnp.sum(jnp.where(named, left_tokens[None], 0), axis=2)
    count_rows = jnp.repeat(count, PAGE_TOKENS, axis=0)
    within = jnp.arange(old_rows, dtype=jnp.int32) % PAGE_TOKENS
    valid = within[:, None] < count_rows
    old_bias = jnp.where(jnp.tile(valid, (1, 2 * GROUP)) & (lanes < steps)[None, :], 0.0, NEG)
    old_bias = old_bias.astype(jnp.float32)

    vmem = pl.BlockSpec(memory_space=pltpu.VMEM)
    f32 = jnp.float32
    out, dec = pl.pallas_call(
        functools.partial(kernel, n),
        out_shape=(
            jax.ShapeDtypeStruct((rows, QUERY_HEADS * HEAD_SIZE), jnp.bfloat16),
            jax.ShapeDtypeStruct((trajs, QUERY_HEADS * HEAD_SIZE), jnp.bfloat16),
        ),
        in_specs=[vmem] * 6,
        out_specs=(vmem, vmem),
        scratch_shapes=[
            pltpu.VMEM((n, CHUNKS, rows, CHUNK_COLS), jnp.bfloat16),
            pltpu.VMEM((QUERY_HEADS, HEAD_SIZE, rows), f32),
            pltpu.VMEM((QUERY_HEADS, 8, rows), f32),
            pltpu.VMEM((QUERY_HEADS, 8, rows), f32),
            pltpu.VMEM((KEY_VALUE_HEADS, HEAD_SIZE, 2 * steps), f32),
            pltpu.VMEM((KEY_VALUE_HEADS, 8, 2 * steps), f32),
            pltpu.VMEM((KEY_VALUE_HEADS, 8, 2 * steps), f32),
            pltpu.VMEM((KEY_VALUE_HEADS, steps, HEAD_SIZE), jnp.bfloat16),
            pltpu.VMEM((KEY_VALUE_HEADS, 2 * steps, HEAD_SIZE), jnp.bfloat16),
            pltpu.VMEM((KEY_VALUE_HEADS, 3, steps, HEAD_SIZE), f32),
            pltpu.VMEM((KEY_VALUE_HEADS, 3, steps, HEAD_SIZE), f32),
            pltpu.SemaphoreType.DMA(((n - 1) * CHUNKS,)),
            pltpu.SemaphoreType.DMA(((n - 1) * CHUNKS,)),
            pltpu.SemaphoreType.DMA((2,)),
            pltpu.SemaphoreType.DMA((2,)),
        ],
        compiler_params=pltpu.CompilerParams(
            collective_id=0, has_side_effects=True, vmem_limit_bytes=44 * 1024 * 1024
        ),
    )(q, kv, pool, dq, bias, old_bias)
    return (out[None], dec)


def solution(mesh):
    placed = (
        P("section", ("groups", "tensor"), None),
        P("section", ("groups", "tensor"), None),
        P(("groups", "tensor", "section"), None),
        P(("groups", "tensor", "section"), None, None),
        P(("groups", "tensor", "section"), None),
        P(("groups", "tensor", "section")),
        P(None, "groups"),
        P(None, "groups"),
    )
    return jax.shard_map(
        on_device,
        mesh=mesh,
        in_specs=placed,
        out_specs=(
            P("section", ("groups", "tensor"), None),
            P(("groups", "tensor", "section"), None),
        ),
        check_vma=False,
    )
```

```python
import functools
import math

import jax
import jax.numpy as jnp
from jax import lax
from jax.experimental import pallas as pl
from jax.experimental.pallas import tpu as pltpu
from jax.sharding import PartitionSpec as P

QUERY_HEADS = 64
KEY_VALUE_HEADS = 8
HEAD_SIZE = 128
PAGE_TOKENS = 4
GROUP = QUERY_HEADS // KEY_VALUE_HEADS
BATCH = 4
NEG = -1e30
EXP2_SCALE = math.log2(math.e) / math.sqrt(HEAD_SIZE)
MESH = pl.DeviceIdType.MESH
CHUNK_HEADS = 2
CHUNKS = KEY_VALUE_HEADS // CHUNK_HEADS
HALF = CHUNKS // 2
CHUNK_COLS = CHUNK_HEADS * 2 * HEAD_SIZE


def ring_place(index, n):
    if n != 8:
        return index
    odd = index % 2
    return (index // 2) * (1 - odd) + (n - 1 - index // 2) * odd


def ring_device(place, n):
    place = (place + 2 * n) % n
    if n != 8:
        return place
    far = place // (n // 2)
    return (2 * place) * (1 - far) + (2 * (n - 1 - place) + 1) * far


def scores_t(k, q):
    return lax.dot_general(k, q, (((1,), (1,)), ((), ())), preferred_element_type=jnp.float32)


def flash(parts, acc_ref, m_ref, l_ref, first):
    tops, alphas, totals, probs = [], [], [], []
    for s, _, h in parts:
        top = jnp.max(s, axis=0, keepdims=True)
        if not first:
            old = m_ref[h, 0:1]
            top = jnp.maximum(top, old)
            alphas.append(jnp.exp2((old - top) * EXP2_SCALE))
        tops.append(top)
    for i, (s, _, h) in enumerate(parts):
        p = jnp.exp2((s - tops[i]) * EXP2_SCALE)
        total = jnp.sum(p, axis=0, keepdims=True)
        totals.append(total if first else total + l_ref[h, 0:1] * alphas[i])
        probs.append(p.astype(jnp.bfloat16))
    mixes = []
    for i, (_, vt, h) in enumerate(parts):
        mix = jnp.dot(vt, probs[i], preferred_element_type=jnp.float32)
        mixes.append(mix if first else mix + acc_ref[h] * alphas[i])
    for i, (_, _, h) in enumerate(parts):
        m_ref[h, 0:1] = tops[i]
        l_ref[h, 0:1] = totals[i]
        acc_ref[h] = mixes[i]


def kernel(
    n,
    q_ref,
    kv_ref,
    pool_ref,
    dq_ref,
    bias_ref,
    old_bias_ref,
    out_ref,
    dec_ref,
    kvs,
    acc,
    m_sc,
    l_sc,
    dacc,
    dm,
    dl,
    dsib,
    dqs,
    xsend,
    xrecv,
    send_sem,
    recv_sem,
    pair_send,
    pair_recv,
):
    rows = q_ref.shape[0]
    steps = dq_ref.shape[1]
    me = lax.axis_index("tensor")
    place = ring_place(me, n)
    right = ring_device(place + 1, n)
    left = ring_device(place - 1, n)
    sibling = 1 - lax.axis_index("section")

    barrier = pltpu.get_barrier_semaphore()
    for target in ({"tensor": right}, {"tensor": left}, {"section": sibling}):
        pl.semaphore_signal(barrier, inc=1, device_id=target, device_id_type=MESH)
    pl.semaphore_wait(barrier, 3)

    def ring_copy(src, slot, chunk, step, target):
        return pltpu.make_async_remote_copy(
            src_ref=src,
            dst_ref=kvs.at[slot, chunk],
            send_sem=send_sem.at[step * CHUNKS + chunk],
            recv_sem=recv_sem.at[step * CHUNKS + chunk],
            device_id={"tensor": target},
            device_id_type=MESH,
        )

    def pair_copy(src, dst, which):
        return pltpu.make_async_remote_copy(
            src_ref=src,
            dst_ref=dst,
            send_sem=pair_send.at[which],
            recv_sem=pair_recv.at[which],
            device_id={"section": sibling},
            device_id_type=MESH,
        )

    for c in range(HALF):
        for chunk, target in ((c, right), (HALF + c, left)):
            kvs[me, chunk] = kv_ref[:, chunk * CHUNK_COLS : (chunk + 1) * CHUNK_COLS]
            ring_copy(kvs.at[me, chunk], me, chunk, 0, target).start()
    swap_queries = pair_copy(dq_ref, dsib, 0)
    swap_queries.start()

    causal = lax.broadcasted_iota(jnp.int32, (rows, rows), 1) >= lax.broadcasted_iota(
        jnp.int32, (rows, rows), 0
    )

    def query_head(h):
        return q_ref[:, pl.ds(pl.multiple_of(h * HEAD_SIZE, HEAD_SIZE), HEAD_SIZE)]

    def attend(k, vt, g, first):
        for start in range(0, GROUP, BATCH):
            parts = []
            for j in range(start, start + BATCH):
                s = scores_t(k, query_head(g * GROUP + j))
                if first:
                    s = jnp.where(causal, s, NEG)
                parts.append((s, vt, g * GROUP + j))
            flash(parts, acc, m_sc, l_sc, first)

    def kv_cols(ref, g):
        start = pl.multiple_of(g * 2 * HEAD_SIZE, 2 * HEAD_SIZE)
        return (
            ref[:, pl.ds(start, HEAD_SIZE)],
            ref[:, pl.ds(pl.multiple_of(start + HEAD_SIZE, HEAD_SIZE), HEAD_SIZE)],
        )

    swap_queries.wait()
    pool_parts = []
    for g in range(KEY_VALUE_HEADS):
        dqs[g, 0:steps] = dq_ref[g]
        dqs[g, steps : 2 * steps] = dsib[g]
        start = g * 2 * HEAD_SIZE
        k = pool_ref[:, start : start + HEAD_SIZE]
        v = pool_ref[:, start + HEAD_SIZE : start + 2 * HEAD_SIZE]
        s = scores_t(k, dqs[g]) + old_bias_ref[...]
        pool_parts.append((s, jnp.transpose(v), g))

    for g in range(0, KEY_VALUE_HEADS, HALF):
        flash(pool_parts[g : g + HALF], dacc, dm, dl, True)

    def own_head(g, carry):
        k, v = kv_cols(kv_ref, g)
        vt = jnp.transpose(v)
        s = scores_t(k, dqs[g]) + bias_ref[me]
        flash([(s, vt, g)], dacc, dm, dl, False)
        attend(k, vt, g, True)
        return carry

    lax.fori_loop(0, KEY_VALUE_HEADS, own_head, 0)

    def ring_step(step, carry):
        src_right = ring_device(place - step, n)
        src_left = ring_device(place + step, n)

        def part(c, carry):
            for chunk, slot, target in ((c, src_right, right), (HALF + c, src_left, left)):
                block = kvs.at[slot, chunk]
                ring_copy(block, slot, chunk, step - 1, target).wait_recv()

                @pl.when(step < n - 1)
                def _():
                    ring_copy(block, slot, chunk, step, target).start()

            parts = []
            for way, slot in ((0, src_right), (1, src_left)):
                mask = bias_ref[slot]
                for inner in range(CHUNK_HEADS):
                    chunk = way * HALF + c
                    start = inner * 2 * HEAD_SIZE
                    k = kvs[slot, chunk, :, start : start + HEAD_SIZE]
                    v = kvs[slot, chunk, :, start + HEAD_SIZE : start + 2 * HEAD_SIZE]
                    g = chunk * CHUNK_HEADS + inner
                    parts.append((scores_t(k, dqs[g]) + mask, jnp.transpose(v), g))
            flash(parts, dacc, dm, dl, False)

            def unit(u, carry):
                way = u // CHUNK_HEADS
                inner = u % CHUNK_HEADS
                chunk = way * HALF + c
                slot = src_right * (1 - way) + src_left * way
                g = chunk * CHUNK_HEADS + inner
                start = pl.multiple_of(inner * 2 * HEAD_SIZE, 2 * HEAD_SIZE)
                k = kvs[slot, chunk, :, pl.ds(start, HEAD_SIZE)]
                v = kvs[
                    slot, chunk, :, pl.ds(pl.multiple_of(start + HEAD_SIZE, HEAD_SIZE), HEAD_SIZE)
                ]
                vt = jnp.transpose(v)
                @pl.when(slot < me)
                def _():
                    k = kvs[slot, chunk, :, pl.ds(start, HEAD_SIZE)]
                    after = pl.multiple_of(start + HEAD_SIZE, HEAD_SIZE)
                    v = kvs[slot, chunk, :, pl.ds(after, HEAD_SIZE)]
                    attend(k, jnp.transpose(v), g, False)

                return carry

            return lax.fori_loop(0, 2 * CHUNK_HEADS, unit, carry)

        return lax.fori_loop(0, HALF, part, carry)

    lax.fori_loop(1, n, ring_step, 0)

    def columns(row):
        return jnp.transpose(jnp.broadcast_to(row, (HEAD_SIZE, 2 * steps)))

    def stage(g, carry):
        xsend[g, 0] = jnp.transpose(dacc[g])[steps:]
        xsend[g, 1] = columns(dm[g, 0:1])[steps:]
        xsend[g, 2] = columns(dl[g, 0:1])[steps:]
        return carry

    lax.fori_loop(0, KEY_VALUE_HEADS, stage, 0)
    swap_parts = pair_copy(xsend, xrecv, 1)
    swap_parts.start()

    def finish(h, carry):
        mix = acc[h] / l_sc[h, 0:1]
        out_ref[:, pl.ds(pl.multiple_of(h * HEAD_SIZE, HEAD_SIZE), HEAD_SIZE)] = jnp.transpose(
            mix
        ).astype(jnp.bfloat16)
        return carry

    lax.fori_loop(0, QUERY_HEADS, finish, 0)
    swap_parts.wait()
    trajs = steps // GROUP
    for g in range(KEY_VALUE_HEADS):
        o_own = jnp.transpose(dacc[g])[:steps]
        m_own = columns(dm[g, 0:1])[:steps]
        l_own = columns(dl[g, 0:1])[:steps]
        top = jnp.maximum(m_own, xrecv[g, 1])
        w_own = jnp.exp2((m_own - top) * EXP2_SCALE)
        w_sib = jnp.exp2((xrecv[g, 1] - top) * EXP2_SCALE)
        mix = (o_own * w_own + xrecv[g, 0] * w_sib) / (l_own * w_own + xrecv[g, 2] * w_sib)
        for j in range(GROUP):
            col = (g * GROUP + j) * HEAD_SIZE
            dec_ref[:, col : col + HEAD_SIZE] = mix[j * trajs : (j + 1) * trajs].astype(
                jnp.bfloat16
            )

    def drain(step, carry):
        for c in range(HALF):
            for chunk, target in ((c, right), (HALF + c, left)):
                ring_copy(kvs.at[me, chunk], me, chunk, step, target).wait_send()
        return carry

    lax.fori_loop(0, n - 1, drain, 0)


def on_device(
    prefill_queries,
    prefill_key_values,
    decode_step_queries,
    cached_page_pool,
    trajectory_page_table,
    lengths,
    page_owner,
    page_slot,
):
    n = lax.axis_size("tensor")
    sections = lax.axis_size("section")
    me = lax.axis_index("tensor")
    section = lax.axis_index("section")
    rows = prefill_queries.shape[1]
    trajs = decode_step_queries.shape[0]
    steps = trajs * GROUP
    old_rows = cached_page_pool.shape[0] * PAGE_TOKENS
    q = prefill_queries[0]
    kv = prefill_key_values[0]
    pool = cached_page_pool.reshape(old_rows, cached_page_pool.shape[2])
    dq = (
        decode_step_queries.reshape(trajs, KEY_VALUE_HEADS, GROUP, HEAD_SIZE)
        .transpose(1, 2, 0, 3)
        .reshape(KEY_VALUE_HEADS, steps, HEAD_SIZE)
    )
    lanes = jnp.arange(2 * steps, dtype=jnp.int32)
    lane_traj = lanes % trajs
    lane_owner = me * sections + jnp.where(lanes < steps, section, 1 - section)
    target = lax.dynamic_index_in_dim(page_owner * trajs + page_slot, section, 0, keepdims=False)
    target = jnp.repeat(target, PAGE_TOKENS)
    bias = jnp.where(
        target[:, None] == (lane_owner * trajs + lane_traj)[None, :], 0.0, NEG
    ).astype(jnp.float32)
    bias = bias.reshape(n, rows, 2 * steps)
    slots = cached_page_pool.shape[0]
    pages = trajectory_page_table.shape[1]
    named = trajectory_page_table[None] == jnp.arange(slots, dtype=jnp.int32)[:, None, None]
    left_tokens = lengths[:, None] - jnp.arange(pages, dtype=jnp.int32)[None, :] * PAGE_TOKENS
    count = jnp.sum(jnp.where(named, left_tokens[None], 0), axis=2)
    count_rows = jnp.repeat(count, PAGE_TOKENS, axis=0)
    within = jnp.arange(old_rows, dtype=jnp.int32) % PAGE_TOKENS
    valid = within[:, None] < count_rows
    old_bias = jnp.where(jnp.tile(valid, (1, 2 * GROUP)) & (lanes < steps)[None, :], 0.0, NEG)
    old_bias = old_bias.astype(jnp.float32)

    vmem = pl.BlockSpec(memory_space=pltpu.VMEM)
    f32 = jnp.float32
    out, dec = pl.pallas_call(
        functools.partial(kernel, n),
        out_shape=(
            jax.ShapeDtypeStruct((rows, QUERY_HEADS * HEAD_SIZE), jnp.bfloat16),
            jax.ShapeDtypeStruct((trajs, QUERY_HEADS * HEAD_SIZE), jnp.bfloat16),
        ),
        in_specs=[vmem] * 6,
        out_specs=(vmem, vmem),
        scratch_shapes=[
            pltpu.VMEM((n, CHUNKS, rows, CHUNK_COLS), jnp.bfloat16),
            pltpu.VMEM((QUERY_HEADS, HEAD_SIZE, rows), f32),
            pltpu.VMEM((QUERY_HEADS, 8, rows), f32),
            pltpu.VMEM((QUERY_HEADS, 8, rows), f32),
            pltpu.VMEM((KEY_VALUE_HEADS, HEAD_SIZE, 2 * steps), f32),
            pltpu.VMEM((KEY_VALUE_HEADS, 8, 2 * steps), f32),
            pltpu.VMEM((KEY_VALUE_HEADS, 8, 2 * steps), f32),
            pltpu.VMEM((KEY_VALUE_HEADS, steps, HEAD_SIZE), jnp.bfloat16),
            pltpu.VMEM((KEY_VALUE_HEADS, 2 * steps, HEAD_SIZE), jnp.bfloat16),
            pltpu.VMEM((KEY_VALUE_HEADS, 3, steps, HEAD_SIZE), f32),
            pltpu.VMEM((KEY_VALUE_HEADS, 3, steps, HEAD_SIZE), f32),
            pltpu.SemaphoreType.DMA(((n - 1) * CHUNKS,)),
            pltpu.SemaphoreType.DMA(((n - 1) * CHUNKS,)),
            pltpu.SemaphoreType.DMA((2,)),
            pltpu.SemaphoreType.DMA((2,)),
        ],
        compiler_params=pltpu.CompilerParams(
            collective_id=0, has_side_effects=True, vmem_limit_bytes=44 * 1024 * 1024
        ),
    )(q, kv, pool, dq, bias, old_bias)
    return (out[None], dec)


def solution(mesh):
    placed = (
        P("section", ("groups", "tensor"), None),
        P("section", ("groups", "tensor"), None),
        P(("groups", "tensor", "section"), None),
        P(("groups", "tensor", "section"), None, None),
        P(("groups", "tensor", "section"), None),
        P(("groups", "tensor", "section")),
        P(None, "groups"),
        P(None, "groups"),
    )
    return jax.shard_map(
        on_device,
        mesh=mesh,
        in_specs=placed,
        out_specs=(
            P("section", ("groups", "tensor"), None),
            P(("groups", "tensor", "section"), None),
        ),
        check_vma=False,
    )
```
